32 devices in a mesh: rows: 8 (over z, y), cols: 4 (over x, core).
Axes of the slice: x: 2, y: 2, z: 4, core: 2. Of those that a mesh axis runs over, the one named last changes fastest.
Arguments:
- tile_values: float32 [120, 256, 256], P('rows'), may hold values from -0.09375 to 0.09375, as said below
- tile_rows: int32 [120], P('rows'), may hold values from 0 to 1
- tile_cols: int32 [120], P('rows'), may hold values from -1 to 15, as said below
- start_vectors: float32 [128, 4096], P('cols', 'rows'), may hold values from -6 to 6
Outputs:
- vectors: float32 [128, 4096], P('cols', 'rows')
- images: float32 [128, 4096], P('cols', 'rows')
The draws below stay inside these ranges and needn't reach their ends.
Inputs may be any that keep to these rules, and one draw needn't show every extreme that they name: tile_values lie within the stated bounds. `tile_cols`: if slot s of index p of rows is not empty, its column block lies on index p + s // 3 - 2 of rows, that is in 2 * (p + s // 3 - 2) up to 2 * (p + s // 3 - 1) - 1; slots whose index would fall off the mesh are empty.
All inputs are finite; a program needn't handle non-finite values.
Results may differ from the reference program's by a relative error of at most 0.0001.
Values sent between devices are 32-bit elements; how exact they have to be, the bound alone decides.
A program may use at most 64 MiB of HBM per device.

```python
import jax
import jax.numpy as jnp
from jax import lax

TILE = 256
K = 128
RB = 2
REACH = 2
GROUP = 3
ITERS = 3
SLOTS = 15
NBLK = 16
BOXES = 4096
NTILES = 120
N_ROWS = 8


def draw_tile_values(key, part):
    slot_index = jnp.arange(NTILES)
    device = (slot_index // SLOTS).astype(jnp.float32)
    scales = 1.0 + 2.0 * device / max(N_ROWS - 1, 1)
    amplitude = 8.0 / TILE
    base = jax.random.uniform(key, (NTILES, TILE, TILE), jnp.float32, -1.0, 1.0)
    return amplitude * scales[:, None, None] * base


def draw_tile_cols(key, part):
    key_count = jax.random.fold_in(key, 11)
    key_slot = jax.random.fold_in(key, 12)
    key_block = jax.random.fold_in(key, 13)
    slot_index = jnp.arange(NTILES, dtype=jnp.int32)
    device = slot_index // SLOTS
    slot_pos = slot_index % SLOTS
    target = device + slot_pos // GROUP - REACH
    live_count = jax.random.randint(key_count, (N_ROWS,), SLOTS // 2, SLOTS + 1)[device]
    slot_draw = jax.random.randint(key_slot, (NTILES,), 0, SLOTS)
    block_pick = jax.random.randint(key_block, (NTILES,), 0, RB)
    is_live = (slot_draw < live_count) & (target >= 0) & (target < N_ROWS)
    return jnp.where(is_live, target * RB + block_pick, -1).astype(jnp.int32)


def place_ends(entries, rng, low, largest):
    shape = entries.shape
    spot = [jax.random.randint(jax.random.fold_in(rng, axis), (), 0, shape[axis]) for axis in range(len(shape))]
    entries = entries.at[tuple(spot)].set(low)
    longest = shape.index(max(shape))
    spot[longest] = (spot[longest] + 1) % shape[longest]
    return entries.at[tuple(spot)].set(largest)


def steps_of(own_key, shape, cuts, smallest, largest):
    def one(dim, blocks):
        steps = jax.random.uniform(jax.random.fold_in(jax.random.fold_in(own_key, 6), dim), (blocks,), jnp.float32, smallest / len(cuts), largest / len(cuts))
        return jnp.repeat(jnp.exp(steps), shape[dim] // blocks).reshape((-1,) + (1,) * (len(shape) - dim - 1))

    level = one(*cuts[0])
    for cut in cuts[1:]:
        level = level * one(*cut)
    return level


def normal_values(key, shape, spread, limit, cuts=(), held_as=jnp.bfloat16):
    entries = jax.random.normal(key, shape, jnp.float32) * spread
    if len(cuts) > 0:
        entries = steps_of(key, shape, cuts, -0.22, 0.18) * entries
    return jnp.clip(entries, min=-limit, max=limit).astype(held_as)


def setup_inputs(seed: int = 0) -> dict:
    key_list = jax.random.split(jax.random.key(seed), 5)
    tile_values = draw_tile_values(jax.random.fold_in(key_list[4], 71), 0)
    tile_rows = place_ends(jax.random.randint(key_list[1], (NTILES,), 0, RB), jax.random.fold_in(key_list[1], 1), 0, RB - 1).astype(jnp.int32)
    tile_cols = draw_tile_cols(jax.random.fold_in(key_list[4], 71), 0)
    start_vectors = normal_values(key_list[3], (K, BOXES), 1.0, 6.0, ((0, 4), (1, 8)), jnp.float32)
    return {"tile_values": tile_values, "tile_rows": tile_rows, "tile_cols": tile_cols, "start_vectors": start_vectors}


highest = lax.Precision.HIGHEST

def reference(tile_values, tile_rows, tile_cols, start_vectors):
    slot_index = jnp.arange(NTILES, dtype=jnp.int32)
    device = slot_index // SLOTS
    is_live = tile_cols >= 0
    row_global = (device * RB + tile_rows).astype(jnp.int32)
    col_global = jnp.where(is_live, tile_cols, 0).astype(jnp.int32)
    weights = is_live.astype(jnp.float32)
    stacked = (tile_values.reshape(N_ROWS, SLOTS, TILE, TILE), row_global.reshape(N_ROWS, SLOTS), col_global.reshape(N_ROWS, SLOTS), weights.reshape(N_ROWS, SLOTS))

    def forward(vectors):
        blocks_in = vectors.reshape(K, NBLK, TILE).transpose(1, 0, 2)

        def visit(totals, item):
            values, rows, cols, mask = item
            chosen = blocks_in[cols]
            product = jnp.einsum('skt,sat->ska', chosen, values, precision=highest) * mask[:, None, None]
            return (totals.at[rows].add(product), None)
        totals, unused = lax.scan(visit, jnp.zeros((NBLK, K, TILE), jnp.float32), stacked)
        return totals.transpose(1, 0, 2).reshape(K, BOXES)

    def adjoint(images):
        blocks_in = images.reshape(K, NBLK, TILE).transpose(1, 0, 2)

        def visit(totals, item):
            values, rows, cols, mask = item
            chosen = blocks_in[rows]
            product = jnp.einsum('ska,sat->skt', chosen, values, precision=highest) * mask[:, None, None]
            return (totals.at[cols].add(product), None)
        totals, unused = lax.scan(visit, jnp.zeros((NBLK, K, TILE), jnp.float32), stacked)
        return totals.transpose(1, 0, 2).reshape(K, BOXES)
    vectors = start_vectors
    images = start_vectors
    for iteration in range(ITERS):
        images = forward(vectors)
        pulled = adjoint(images)
        gram_full = jnp.dot(pulled, pulled.T, precision=highest)
        factor = jnp.linalg.cholesky(gram_full)
        inverse = jax.scipy.linalg.solve_triangular(factor, jnp.eye(K, dtype=jnp.float32), lower=True)
        vectors = jnp.sqrt(jnp.float32(BOXES)) * jnp.dot(inverse, pulled, precision=highest)
    return (vectors, images)
```

```python
import functools

import jax
import jax.numpy as jnp
from jax import lax
from jax.experimental import pallas as pl
from jax.experimental.pallas import tpu as pltpu
from jax.sharding import PartitionSpec as P

REACH = 2
ITERS = 3
PARTS = 3
SUB = 8
GROUPS = 2 * REACH + 1
MESH = pl.DeviceIdType.MESH
F32 = jnp.float32
BF16 = jnp.bfloat16


def split(x, parts):
    out = []
    for part in range(parts):
        piece = x.astype(BF16)
        out.append(piece)
        if part < parts - 1:
            x = x - piece.astype(F32)
    return out


def dot(a, b, dims):
    return lax.dot_general(a, b, (dims, ((), ())), preferred_element_type=F32)


def dot32(a, b, dims):
    return lax.dot_general(
        a, b, (dims, ((), ())), precision=lax.Precision.HIGHEST, preferred_element_type=F32
    )


def wait_bytes(ref, sem):
    pltpu.make_async_copy(ref, ref, sem).wait()


def factor_step(m_ref, step):
    size = m_ref.shape[0]
    base = pl.multiple_of(step * SUB, SUB)
    lane = lax.broadcasted_iota(jnp.int32, (SUB, size), 1) - base
    row = lax.broadcasted_iota(jnp.int32, (SUB, size), 0)
    band = m_ref[pl.ds(base, SUB), :]
    turned = pltpu.roll(band, lax.rem(size - base, size), 1)
    cols = [jnp.broadcast_to(turned[:, k : k + 1], (SUB, size)) for k in range(SUB)]
    inverse_rows = jnp.zeros((SUB, size), F32)
    for k in range(SUB):
        inverse = 1.0 / jnp.broadcast_to(cols[k][k : k + 1, :], (SUB, size))
        inverse_rows = jnp.where(row == k, inverse, inverse_rows)
        if k < SUB - 1:
            scale = jnp.where(row > k, cols[k] * inverse, 0.0)
            for other in range(k + 1, SUB):
                cols[other] = cols[other] - scale * cols[other][k : k + 1, :]
            pivot = jnp.where(lane[:1] == k, 1.0, band[k : k + 1, :])
            band = jnp.where((lane == k) & (row > k), 0.0, band) - scale * pivot
    right = jnp.where(lane == row, 1.0, jnp.where((lane > row) & (lane < SUB), 0.0, band))
    left = jnp.where(lane >= SUB, band * inverse_rows, 0.0)
    left_parts = [part.astype(F32) for part in split(left, 3)]
    right_parts = [part.astype(F32) for part in split(right, 3)]
    pairs = [(0, 0), (0, 1), (1, 0), (1, 1), (0, 2), (2, 0)]
    left_all = jnp.concatenate([left_parts[a] for a, b in pairs], axis=0).astype(BF16)
    right_all = jnp.concatenate([right_parts[b] for a, b in pairs], axis=0).astype(BF16)
    change = dot(left_all, right_all, ((0,), (0,)))
    whole_lane = lax.broadcasted_iota(jnp.int32, (size, size), 1) - base
    whole_row = lax.broadcasted_iota(jnp.int32, (size, size), 0) - base
    cleared = (whole_row >= SUB) & (whole_lane >= 0) & (whole_lane < SUB)
    m_ref[...] = jnp.where(cleared, 0.0, m_ref[...]) - change
    m_ref[pl.ds(base, SUB), :] = band


def inverse_factor(m_ref, scale):
    size = m_ref.shape[0]

    def step(index, carry):
        factor_step(m_ref, index)
        return carry

    lax.fori_loop(0, size // SUB, step, 0)
    lane = lax.broadcasted_iota(jnp.int32, (size, size), 1)
    row = lax.broadcasted_iota(jnp.int32, (size, size), 0)
    whole = m_ref[...]
    pivots = jnp.sum(jnp.where(lane == row, whole, 0.0), axis=1, keepdims=True)
    unit = jnp.where(lane == row, 1.0, jnp.where(lane < row, whole, 0.0))
    m_ref[...] = unit * (scale / jnp.sqrt(pivots))


def kernel(
    n_rows, n_cols, scale,
    tiles_hbm, tile_rows, tile_cols, start,
    vectors_out, images_out,
    tiles, dense, source, window, terms, landed, gram, collected, whole_gram, all_images, all_pulled,
    tile_sem, window_send, window_recv, terms_send, terms_recv,
    reduce_send, reduce_recv, spread_send, spread_recv, last_send, last_recv,
):
    p, c = lax.axis_index("rows"), lax.axis_index("cols")
    n_devices = n_rows * n_cols
    me = p * n_cols + c
    local, width = start.shape
    piece = width // n_cols
    size = local * n_cols
    blocks = 2
    tile = tiles.shape[1]
    in_group = tiles.shape[0] // GROUPS
    reducers = size // SUB
    stride = n_devices // reducers
    is_reducer = lax.rem(me, stride) == 0

    def at(row, col):
        return {"rows": row, "cols": col}

    def flat(index):
        return at(index // n_cols, lax.rem(index, n_cols))

    def valid(group):
        there = p + group - REACH
        return (there >= 0) & (there < n_rows)

    def copy_of_tiles(group):
        part = pl.ds(group * in_group, in_group)
        return pltpu.make_async_copy(tiles_hbm.at[part], tiles.at[part], tile_sem.at[group])

    for group in range(GROUPS):
        copy_of_tiles(group).start()

    barrier = pltpu.get_barrier_semaphore()

    def greet(index, carry):
        @pl.when(index != me)
        def _():
            pl.semaphore_signal(barrier, inc=1, device_id=flat(index), device_id_type=MESH)

        return carry

    lax.fori_loop(0, n_devices, greet, 0)

    for part in range(n_cols):
        source[0, part] = start[:, part * piece : (part + 1) * piece]
    for group in range(GROUPS):

        @pl.when(jnp.logical_not(valid(group)))
        def _():
            for iteration in range(ITERS):
                part = pl.ds(group * n_cols, n_cols)
                window[iteration, part] = jnp.zeros((n_cols, local, piece), F32)
                terms[iteration, part] = jnp.zeros((n_cols, local, piece), F32)

    pl.semaphore_wait(barrier, n_devices - 1)

    for group in range(GROUPS):
        mirror = GROUPS - 1 - group
        there = window.at[0, pl.ds(mirror * n_cols, n_cols)]
        if group == REACH:
            pltpu.make_async_copy(source.at[0], there, window_recv.at[0, mirror]).start()
        else:

            @pl.when(valid(group))
            def _():
                pltpu.make_async_remote_copy(
                    src_ref=source.at[0],
                    dst_ref=there,
                    send_sem=window_send.at[0, group],
                    recv_sem=window_recv.at[0, mirror],
                    device_id=at(p + group - REACH, c),
                    device_id_type=MESH,
                ).start()

    chunk = 32
    chunks = tile // chunk
    for group in range(GROUPS):
        copy_of_tiles(group).wait()
        weights = []
        for r in range(blocks):
            for b in range(blocks):
                for s in range(in_group):
                    slot = group * in_group + s
                    hit = (tile_rows[slot] == r) & (lax.rem(tile_cols[slot], blocks) == b)
                    weights.append(jnp.where(hit, 1.0, 0.0).astype(F32))

        def build(index, carry):
            start_row = pl.multiple_of(index * chunk, chunk)
            values = [tiles[group * in_group + s, pl.ds(start_row, chunk), :] for s in range(in_group)]
            for r in range(blocks):
                for b in range(blocks):
                    first = (r * blocks + b) * in_group
                    total = values[0] * weights[first]
                    for s in range(1, in_group):
                        total = total + values[s] * weights[first + s]
                    for number, part in enumerate(split(total, PARTS)):
                        dense[number, group, pl.ds(r * tile + start_row, chunk), b * tile : (b + 1) * tile] = part
            return carry

        lax.fori_loop(0, chunks, build, 0)

    def product(x, group, dims):
        parts = split(x, PARTS)
        total = None
        for number in range(PARTS):
            count = PARTS - number
            stacked = jnp.concatenate(parts[:count], axis=0)
            result = dot(stacked, dense[number, group], dims)
            for k in range(count):
                term = result[k * local : (k + 1) * local]
                total = term if total is None else total + term
        return total

    def send_pieces(iteration, group, buffer, sources, first, send, recv):
        mirror = GROUPS - 1 - group
        slot = mirror * n_cols + c
        for col in range(n_cols):

            def remote():
                pltpu.make_async_remote_copy(
                    src_ref=sources.at[first + col],
                    dst_ref=buffer.at[iteration, slot],
                    send_sem=send.at[iteration, group],
                    recv_sem=recv.at[iteration, mirror],
                    device_id=at(p + group - REACH, col),
                    device_id_type=MESH,
                ).start()

            if group == REACH:
                pl.when(col != c)(remote)

                @pl.when(col == c)
                def _():
                    pltpu.make_async_copy(
                        sources.at[first + col], buffer.at[iteration, slot], recv.at[iteration, mirror]
                    ).start()
            else:
                pl.when(valid(group))(remote)

    def spread_over_cols(src, buffer, number):
        for col in range(n_cols):

            @pl.when(col != c)
            def _():
                pltpu.make_async_remote_copy(
                    src_ref=src,
                    dst_ref=buffer.at[c],
                    send_sem=last_send.at[number],
                    recv_sem=last_recv.at[number],
                    device_id=at(p, col),
                    device_id_type=MESH,
                ).start()

            @pl.when(col == c)
            def _():
                pltpu.make_async_copy(src, buffer.at[c], last_recv.at[number]).start()

    order = [group for group in range(GROUPS) if group != REACH]
    order = sorted(order, key=lambda group: -abs(group - REACH)) + [REACH]

    def wait_group(buffer, recv, iteration, group):
        part = buffer.at[iteration, pl.ds(group * n_cols, n_cols)]
        pl.when(valid(group))(lambda: wait_bytes(part, recv.at[iteration, group]))

    def images_and_terms(iteration):
        images = jnp.zeros((local, width), F32)
        for group in reversed(order):
            wait_group(window, window_recv, iteration, group)
            near = jnp.concatenate([window[iteration, group * n_cols + k] for k in range(n_cols)], axis=1)
            images = images + product(near, group, ((1,), (1,)))
        if iteration == ITERS - 1:
            images_out[...] = images
            spread_over_cols(images_out, all_images, 0)
        for group in order:
            pulled = product(images, group, ((1,), (0,)))
            for col in range(n_cols):
                landed[iteration, group * n_cols + col] = pulled[:, col * piece : (col + 1) * piece]
            send_pieces(
                iteration, group, terms, landed.at[iteration], group * n_cols, terms_send, terms_recv
            )

    def pull(iteration):
        total = None
        for group in order:
            wait_group(terms, terms_recv, iteration, group)
            part = terms[iteration, group * n_cols : (group + 1) * n_cols].reshape(size, piece)
            total = part if total is None else total + part
        return total

    def start_gram(iteration, pulled):
        gram[iteration] = dot32(pulled, pulled, ((1,), (1,)))

        def send(index, carry):
            part = gram.at[iteration, pl.ds(pl.multiple_of(index * SUB, SUB), SUB)]

            @pl.when(index * stride != me)
            def _():
                pltpu.make_async_remote_copy(
                    src_ref=part,
                    dst_ref=collected.at[iteration, me],
                    send_sem=reduce_send.at[iteration],
                    recv_sem=reduce_recv.at[iteration],
                    device_id=flat(index * stride),
                    device_id_type=MESH,
                ).start()

            @pl.when(index * stride == me)
            def _():
                pltpu.make_async_copy(part, collected.at[iteration, me], reduce_recv.at[iteration]).start()

            return carry

        lax.fori_loop(0, reducers, send, 0)

    def spread_gram(iteration):
        @pl.when(is_reducer)
        def _():
            wait_bytes(collected.at[iteration], reduce_recv.at[iteration])
            mine = pl.ds(pl.multiple_of(me // stride * SUB, SUB), SUB)
            whole_gram[ITERS + iteration, mine] = jnp.sum(collected[iteration], axis=0)
            part = whole_gram.at[ITERS + iteration, mine]
            target = whole_gram.at[iteration, mine]

            def send(index, carry):
                @pl.when(index != me)
                def _():
                    pltpu.make_async_remote_copy(
                        src_ref=part,
                        dst_ref=target,
                        send_sem=spread_send.at[iteration],
                        recv_sem=spread_recv.at[iteration],
                        device_id=flat(index),
                        device_id_type=MESH,
                    ).start()

                return carry

            pltpu.make_async_copy(part, target, spread_recv.at[iteration]).start()
            lax.fori_loop(0, n_devices, send, 0)

    def factor(iteration):
        wait_bytes(whole_gram.at[iteration], spread_recv.at[iteration])
        inverse_factor(whole_gram.at[iteration], scale)

    for iteration in range(ITERS):
        if iteration > 0:
            spread_gram(iteration - 1)
        images_and_terms(iteration)
        if iteration > 0:
            factor(iteration - 1)
        pulled = pull(iteration)
        if iteration > 0:
            pulled = dot32(whole_gram[iteration - 1], pulled, ((1,), (0,)))
        source[iteration + 1] = pulled.reshape(n_cols, local, piece)
        if iteration < ITERS - 1:
            for group in order:
                send_pieces(
                    iteration + 1, group, window, source.at[iteration + 1], 0, window_send, window_recv
                )
        start_gram(iteration, pulled)
        if iteration == ITERS - 1:
            spread_over_cols(source.at[ITERS], all_pulled, 1)

    spread_gram(ITERS - 1)
    own = pl.ds(pl.multiple_of(c * local, local), local)
    wait_bytes(all_images, last_recv.at[0])
    wait_bytes(all_images.at[pl.ds(0, n_cols - 1)], last_send.at[0])
    images_out[...] = dot32(
        whole_gram[ITERS - 2, own], all_images[...].reshape(size, width), ((1,), (0,))
    )
    factor(ITERS - 1)
    wait_bytes(all_pulled, last_recv.at[1])
    mix = whole_gram[ITERS - 1, own]
    for part in range(n_cols):
        vectors_out[:, part * piece : (part + 1) * piece] = dot32(
            mix, all_pulled[part].reshape(size, piece), ((1,), (0,))
        )

    wait_bytes(all_pulled.at[pl.ds(0, n_cols - 1)], last_send.at[1])
    for iteration in range(ITERS):
        for group in range(GROUPS):
            for buffer, send in ((window, window_send), (terms, terms_send)):
                if group == REACH:
                    if buffer is window and iteration == 0:
                        continue
                    part = buffer.at[iteration, pl.ds(0, n_cols - 1)]
                    wait_bytes(part, send.at[iteration, group])
                else:
                    part = buffer.at[iteration, pl.ds(0, n_cols)]
                    pl.when(valid(group))(functools.partial(wait_bytes, part, send.at[iteration, group]))

        @pl.when(is_reducer)
        def _():
            wait_bytes(gram.at[iteration, pl.ds(0, size - SUB)], reduce_send.at[iteration])
            wait_bytes(collected.at[iteration, pl.ds(0, n_devices - 1)], spread_send.at[iteration])

        @pl.when(jnp.logical_not(is_reducer))
        def _():
            wait_bytes(gram.at[iteration], reduce_send.at[iteration])


def solution(mesh):
    n_rows, n_cols = mesh.shape["rows"], mesh.shape["cols"]

    def body(tile_values, tile_rows, tile_cols, start_vectors):
        slots, tile = tile_values.shape[:2]
        local, width = start_vectors.shape
        size, piece = local * n_cols, width // n_cols
        scale = float((width * n_rows) ** 0.5)
        pieces = (ITERS, GROUPS * n_cols, local, piece)
        dma = pltpu.SemaphoreType.DMA
        vmem = pl.BlockSpec(memory_space=pltpu.VMEM)
        smem = pl.BlockSpec(memory_space=pltpu.SMEM)
        out = jax.ShapeDtypeStruct((local, width), F32)
        return pl.pallas_call(
            functools.partial(kernel, n_rows, n_cols, scale),
            out_shape=(out, out),
            in_specs=[pl.BlockSpec(memory_space=pl.ANY), smem, smem, vmem],
            out_specs=(vmem, vmem),
            scratch_shapes=[
                pltpu.VMEM((slots, tile, tile), F32),
                pltpu.VMEM((PARTS, GROUPS, width, width), BF16),
                pltpu.VMEM((ITERS + 1, n_cols, local, piece), F32),
                pltpu.VMEM(pieces, F32),
                pltpu.VMEM(pieces, F32),
                pltpu.VMEM(pieces, F32),
                pltpu.VMEM((ITERS, size, size), F32),
                pltpu.VMEM((ITERS, n_rows * n_cols, SUB, size), F32),
                pltpu.VMEM((2 * ITERS, size, size), F32),
                pltpu.VMEM((n_cols, local, width), F32),
                pltpu.VMEM((n_cols, n_cols, local, piece), F32),
                dma((GROUPS,)),
                dma((ITERS, GROUPS)),
                dma((ITERS, GROUPS)),
                dma((ITERS, GROUPS)),
                dma((ITERS, GROUPS)),
                dma((ITERS,)),
                dma((ITERS,)),
                dma((ITERS,)),
                dma((ITERS,)),
                dma((2,)),
                dma((2,)),
            ],
            compiler_params=pltpu.CompilerParams(
                collective_id=0, has_side_effects=True, vmem_limit_bytes=48 * 1024 * 1024
            ),
        )(tile_values, tile_rows, tile_cols, start_vectors)

    return jax.shard_map(
        body,
        mesh=mesh,
        in_specs=(P("rows", None, None), P("rows"), P("rows"), P("cols", "rows")),
        out_specs=(P("cols", "rows"), P("cols", "rows")),
        check_vma=False,
    )
```

```python
import functools

import jax
import jax.numpy as jnp
from jax import lax
from jax.experimental import pallas as pl
from jax.experimental.pallas import tpu as pltpu
from jax.sharding import PartitionSpec as P

REACH = 2
ITERS = 3
PARTS = 2
SUB = 8
GROUPS = 2 * REACH + 1
MESH = pl.DeviceIdType.MESH
F32 = jnp.float32
BF16 = jnp.bfloat16


def split(x, parts):
    out = []
    for part in range(parts):
        piece = x.astype(BF16)
        out.append(piece)
        if part < parts - 1:
            x = x - piece.astype(F32)
    return out


def dot(a, b, dims):
    return lax.dot_general(a, b, (dims, ((), ())), preferred_element_type=F32)


def dot32(a, b, dims):
    return lax.dot_general(
        a, b, (dims, ((), ())), precision=lax.Precision.HIGHEST, preferred_element_type=F32
    )


def wait_bytes(ref, sem):
    pltpu.make_async_copy(ref, ref, sem).wait()


def inverse_factor(whole, scale):
    size = whole.shape[0]
    count = size // SUB
    bands = [whole[s * SUB : (s + 1) * SUB] for s in range(count)]
    lane = lax.broadcasted_iota(jnp.int32, (SUB, size), 1)
    row = lax.broadcasted_iota(jnp.int32, (SUB, size), 0)
    full = (SUB, size)
    result = []
    for s in range(count):
        base = s * SUB
        band = bands[s]
        cols = [jnp.broadcast_to(band[:, base + k : base + k + 1], full) for k in range(SUB)]
        entry = {
            (k, l): jnp.broadcast_to(cols[l][k : k + 1], full) for k in range(SUB) for l in range(k, SUB)
        }
        follows = s + 1 < count
        if follows:
            below = bands[s + 1]
            below_cols = [jnp.broadcast_to(below[:, base + k : base + k + 1], full) for k in range(SUB)]
        inverse_rows = jnp.zeros(full, F32)
        pivots = jnp.zeros(full, F32)
        for k in range(SUB):
            inverse = pl.reciprocal(entry[k, k])
            pivots = jnp.where(row == k, entry[k, k], pivots)
            inverse_rows = jnp.where(row == k, inverse, inverse_rows)
            factors = {l: entry[k, l] * inverse for l in range(k + 1, SUB)}
            for l in range(k + 1, SUB):
                for j in range(l, SUB):
                    entry[l, j] = entry[l, j] - factors[l] * entry[k, j]
            here = lane == base + k
            pivot_row = jnp.where(here, 1.0, jnp.broadcast_to(band[k : k + 1], full))
            if k < SUB - 1:
                step = jnp.where(row > k, cols[k] * inverse, 0.0)
                for l in range(k + 1, SUB):
                    cols[l] = cols[l] - step * entry[k, l]
                band = jnp.where(here & (row > k), 0.0, band) - step * pivot_row
            if follows:
                step = below_cols[k] * inverse
                for l in range(k + 1, SUB):
                    below_cols[l] = below_cols[l] - step * entry[k, l]
                below = jnp.where(here, 0.0, below) - step * pivot_row
        if follows:
            bands[s + 1] = below
        offset = lane - base
        if s + 2 < count:
            right = jnp.where(offset == row, 1.0, jnp.where((offset > row) & (offset < SUB), 0.0, band))
            left_parts = [part.astype(F32) for part in split(band * inverse_rows, 3)]
            right_parts = [part.astype(F32) for part in split(right, 3)]
            pairs = [(0, 0), (0, 1), (1, 0), (1, 1), (0, 2), (2, 0)]
            left_all = jnp.concatenate([left_parts[a] for a, b in pairs], axis=0).astype(BF16)
            right_all = jnp.concatenate([right_parts[b] for a, b in pairs], axis=0).astype(BF16)
            change = dot(left_all, right_all, ((0,), (0,)))
            inside = (offset >= 0) & (offset < SUB)
            for i in range(s + 2, count):
                bands[i] = jnp.where(inside, 0.0, bands[i]) - change[i * SUB : (i + 1) * SUB]
        unit = jnp.where(offset == row, 1.0, jnp.where(offset < row, band, 0.0))
        result.append(unit * (scale / jnp.sqrt(pivots)))
    return jnp.concatenate(result, axis=0)


def kernel(
    n_rows, n_cols, scale,
    tiles_hbm, rows_hbm, cols_hbm, start,
    vectors_out, images_out,
    tiles, dense, source, window, terms, landed, gram, collected, whole_gram, all_images, all_pulled,
    tile_rows, tile_cols, tile_sem, input_sem, window_send, window_recv, terms_send, terms_recv,
    reduce_send, reduce_recv, spread_send, spread_recv, last_send, last_recv,
):
    p, c = lax.axis_index("rows"), lax.axis_index("cols")
    n_devices = n_rows * n_cols
    me = p * n_cols + c
    local, width = start.shape
    piece = width // n_cols
    size = local * n_cols
    blocks = 2
    tile = tiles.shape[1]
    in_group = tiles.shape[0] // GROUPS
    reducers = size // SUB
    stride = n_devices // reducers
    is_reducer = lax.rem(me, stride) == 0

    def at(row, col):
        return {"rows": row, "cols": col}

    def flat(index):
        return at(index // n_cols, lax.rem(index, n_cols))

    def valid(group):
        there = p + group - REACH
        return (there >= 0) & (there < n_rows)

    def copy_of_tiles(group):
        part = pl.ds(group * in_group, in_group)
        return pltpu.make_async_copy(tiles_hbm.at[part], tiles.at[part], tile_sem.at[group])

    for group in range(GROUPS):
        copy_of_tiles(group).start()

    inputs = [
        pltpu.make_async_copy(start.at[:, pl.ds(part * piece, piece)], source.at[0, part], input_sem.at[part])
        for part in range(n_cols)
    ]
    tables = [
        pltpu.make_async_copy(rows_hbm, tile_rows, input_sem.at[n_cols]),
        pltpu.make_async_copy(cols_hbm, tile_cols, input_sem.at[n_cols + 1]),
    ]
    for copy in inputs + tables:
        copy.start()

    barrier = pltpu.get_barrier_semaphore()

    def greet(index, carry):
        @pl.when(index != me)
        def _():
            pl.semaphore_signal(barrier, inc=1, device_id=flat(index), device_id_type=MESH)

        return carry

    lax.fori_loop(0, n_devices, greet, 0)

    for group in range(GROUPS):

        @pl.when(jnp.logical_not(valid(group)))
        def _():
            for iteration in range(ITERS):
                part = pl.ds(group * n_cols, n_cols)
                window[iteration, part] = jnp.zeros((n_cols, local, piece), F32)
                terms[iteration, part] = jnp.zeros((n_cols, local, piece), F32)

    for copy in inputs:
        copy.wait()
    pl.semaphore_wait(barrier, n_devices - 1)

    for group in range(GROUPS):
        mirror = GROUPS - 1 - group
        there = window.at[0, pl.ds(mirror * n_cols, n_cols)]
        if group == REACH:
            pltpu.make_async_copy(source.at[0], there, window_recv.at[0, mirror]).start()
        else:

            @pl.when(valid(group))
            def _():
                pltpu.make_async_remote_copy(
                    src_ref=source.at[0],
                    dst_ref=there,
                    send_sem=window_send.at[0, group],
                    recv_sem=window_recv.at[0, mirror],
                    device_id=at(p + group - REACH, c),
                    device_id_type=MESH,
                ).start()

    for copy in tables:
        copy.wait()
    chunk = 32
    chunks = tile // chunk
    for group in range(GROUPS):
        copy_of_tiles(group).wait()
        weights = []
        for r in range(blocks):
            for b in range(blocks):
                for s in range(in_group):
                    slot = group * in_group + s
                    hit = (tile_rows[slot] == r) & (lax.rem(tile_cols[slot], blocks) == b)
                    weights.append(jnp.where(hit, 1.0, 0.0).astype(F32))

        def build(index, carry):
            start_row = pl.multiple_of(index * chunk, chunk)
            values = [tiles[group * in_group + s, pl.ds(start_row, chunk), :] for s in range(in_group)]
            for r in range(blocks):
                for b in range(blocks):
                    first = (r * blocks + b) * in_group
                    total = values[0] * weights[first]
                    for s in range(1, in_group):
                        total = total + values[s] * weights[first + s]
                    for number, part in enumerate(split(total, PARTS)):
                        dense[number, group, pl.ds(r * tile + start_row, chunk), b * tile : (b + 1) * tile] = part
            return carry

        lax.fori_loop(0, chunks, build, 0)

    def product(x, group, dims):
        parts = split(x, PARTS)
        total = None
        for number in range(PARTS):
            count = PARTS
            stacked = jnp.concatenate(parts[:count], axis=0)
            result = dot(stacked, dense[number, group], dims)
            for k in range(count):
                term = result[k * local : (k + 1) * local]
                total = term if total is None else total + term
        return total

    def send_pieces(iteration, group, buffer, sources, first, send, recv):
        mirror = GROUPS - 1 - group
        slot = mirror * n_cols + c
        for col in range(n_cols):

            def remote():
                pltpu.make_async_remote_copy(
                    src_ref=sources.at[first + col],
                    dst_ref=buffer.at[iteration, slot],
                    send_sem=send.at[iteration, group],
                    recv_sem=recv.at[iteration, mirror],
                    device_id=at(p + group - REACH, col),
                    device_id_type=MESH,
                ).start()

            if group == REACH:
                pl.when(col != c)(remote)

                @pl.when(col == c)
                def _():
                    pltpu.make_async_copy(
                        sources.at[first + col], buffer.at[iteration, slot], recv.at[iteration, mirror]
                    ).start()
            else:
                pl.when(valid(group))(remote)

    def spread_over_cols(src, buffer, number):
        for col in range(n_cols):

            @pl.when(col != c)
            def _():
                pltpu.make_async_remote_copy(
                    src_ref=src,
                    dst_ref=buffer.at[c],
                    send_sem=last_send.at[number],
                    recv_sem=last_recv.at[number],
                    device_id=at(p, col),
                    device_id_type=MESH,
                ).start()

            @pl.when(col == c)
            def _():
                pltpu.make_async_copy(src, buffer.at[c], last_recv.at[number]).start()

    order = [group for group in range(GROUPS) if group != REACH]
    order = sorted(order, key=lambda group: -abs(group - REACH)) + [REACH]

    def wait_group(buffer, recv, iteration, group):
        part = buffer.at[iteration, pl.ds(group * n_cols, n_cols)]
        pl.when(valid(group))(lambda: wait_bytes(part, recv.at[iteration, group]))

    def images_and_terms(iteration):
        images = jnp.zeros((local, width), F32)
        for group in reversed(order):
            wait_group(window, window_recv, iteration, group)
            near = jnp.concatenate([window[iteration, group * n_cols + k] for k in range(n_cols)], axis=1)
            images = images + product(near, group, ((1,), (1,)))
        if iteration == ITERS - 1:
            images_out[...] = images
            spread_over_cols(images_out, all_images, 0)
        for group in order:
            pulled = product(images, group, ((1,), (0,)))
            for col in range(n_cols):
                landed[iteration, group * n_cols + col] = pulled[:, col * piece : (col + 1) * piece]
            send_pieces(
                iteration, group, terms, landed.at[iteration], group * n_cols, terms_send, terms_recv
            )

    def pull(iteration):
        total = None
        for group in order:
            wait_group(terms, terms_recv, iteration, group)
            part = terms[iteration, group * n_cols : (group + 1) * n_cols].reshape(size, piece)
            total = part if total is None else total + part
        return total

    def start_gram(iteration, pulled):
        gram[iteration] = dot32(pulled, pulled, ((1,), (1,)))

        def send(index, carry):
            part = gram.at[iteration, pl.ds(pl.multiple_of(index * SUB, SUB), SUB)]

            @pl.when(index * stride != me)
            def _():
                pltpu.make_async_remote_copy(
                    src_ref=part,
                    dst_ref=collected.at[iteration, me],
                    send_sem=reduce_send.at[iteration],
                    recv_sem=reduce_recv.at[iteration],
                    device_id=flat(index * stride),
                    device_id_type=MESH,
                ).start()

            @pl.when(index * stride == me)
            def _():
                pltpu.make_async_copy(part, collected.at[iteration, me], reduce_recv.at[iteration]).start()

            return carry

        lax.fori_loop(0, reducers, send, 0)

    def spread_gram(iteration):
        @pl.when(is_reducer)
        def _():
            wait_bytes(collected.at[iteration], reduce_recv.at[iteration])
            mine = pl.ds(pl.multiple_of(me // stride * SUB, SUB), SUB)
            whole_gram[ITERS + iteration, mine] = jnp.sum(collected[iteration], axis=0)
            part = whole_gram.at[ITERS + iteration, mine]
            target = whole_gram.at[iteration, mine]

            def send(index, carry):
                @pl.when(index != me)
                def _():
                    pltpu.make_async_remote_copy(
                        src_ref=part,
                        dst_ref=target,
                        send_sem=spread_send.at[iteration],
                        recv_sem=spread_recv.at[iteration],
                        device_id=flat(index),
                        device_id_type=MESH,
                    ).start()

                return carry

            pltpu.make_async_copy(part, target, spread_recv.at[iteration]).start()
            lax.fori_loop(0, n_devices, send, 0)

    def factor(iteration):
        wait_bytes(whole_gram.at[iteration], spread_recv.at[iteration])
        whole_gram[iteration] = inverse_factor(whole_gram[iteration], scale)

    for iteration in range(ITERS):
        if iteration > 0:
            spread_gram(iteration - 1)
        images_and_terms(iteration)
        if iteration > 0:
            factor(iteration - 1)
        pulled = pull(iteration)
        if iteration > 0:
            pulled = dot32(whole_gram[iteration - 1], pulled, ((1,), (0,)))
        source[iteration + 1] = pulled.reshape(n_cols, local, piece)
        if iteration < ITERS - 1:
            for group in order:
                send_pieces(
                    iteration + 1, group, window, source.at[iteration + 1], 0, window_send, window_recv
                )
        start_gram(iteration, pulled)
        if iteration == ITERS - 1:
            spread_over_cols(source.at[ITERS], all_pulled, 1)

    spread_gram(ITERS - 1)
    own = pl.ds(pl.multiple_of(c * local, local), local)
    wait_bytes(all_images, last_recv.at[0])
    wait_bytes(all_images.at[pl.ds(0, n_cols - 1)], last_send.at[0])
    images_out[...] = dot32(
        whole_gram[ITERS - 2, own], all_images[...].reshape(size, width), ((1,), (0,))
    )
    factor(ITERS - 1)
    wait_bytes(all_pulled, last_recv.at[1])
    mix = whole_gram[ITERS - 1, own]
    for part in range(n_cols):
        vectors_out[:, part * piece : (part + 1) * piece] = dot32(
            mix, all_pulled[part].reshape(size, piece), ((1,), (0,))
        )

    wait_bytes(all_pulled.at[pl.ds(0, n_cols - 1)], last_send.at[1])
    for iteration in range(ITERS):
        for group in range(GROUPS):
            for buffer, send in ((window, window_send), (terms, terms_send)):
                if group == REACH:
                    if buffer is window and iteration == 0:
                        continue
                    part = buffer.at[iteration, pl.ds(0, n_cols - 1)]
                    wait_bytes(part, send.at[iteration, group])
                else:
                    part = buffer.at[iteration, pl.ds(0, n_cols)]
                    pl.when(valid(group))(functools.partial(wait_bytes, part, send.at[iteration, group]))

        @pl.when(is_reducer)
        def _():
            wait_bytes(gram.at[iteration, pl.ds(0, size - SUB)], reduce_send.at[iteration])
            wait_bytes(collected.at[iteration, pl.ds(0, n_devices - 1)], spread_send.at[iteration])

        @pl.when(jnp.logical_not(is_reducer))
        def _():
            wait_bytes(gram.at[iteration], reduce_send.at[iteration])


def solution(mesh):
    n_rows, n_cols = mesh.shape["rows"], mesh.shape["cols"]

    def body(tile_values, tile_rows, tile_cols, start_vectors):
        slots, tile = tile_values.shape[:2]
        local, width = start_vectors.shape
        size, piece = local * n_cols, width // n_cols
        scale = float((width * n_rows) ** 0.5)
        pieces = (ITERS, GROUPS * n_cols, local, piece)
        dma = pltpu.SemaphoreType.DMA
        vmem = pl.BlockSpec(memory_space=pltpu.VMEM)
        hbm = pl.BlockSpec(memory_space=pltpu.HBM)
        out = jax.ShapeDtypeStruct((local, width), F32)
        return pl.pallas_call(
            functools.partial(kernel, n_rows, n_cols, scale),
            out_shape=(out, out),
            in_specs=[hbm, hbm, hbm, hbm],
            out_specs=(vmem, vmem),
            scratch_shapes=[
                pltpu.VMEM((slots, tile, tile), F32),
                pltpu.VMEM((PARTS, GROUPS, width, width), BF16),
                pltpu.VMEM((ITERS + 1, n_cols, local, piece), F32),
                pltpu.VMEM(pieces, F32),
                pltpu.VMEM(pieces, F32),
                pltpu.VMEM(pieces, F32),
                pltpu.VMEM((ITERS, size, size), F32),
                pltpu.VMEM((ITERS, n_rows * n_cols, SUB, size), F32),
                pltpu.VMEM((2 * ITERS, size, size), F32),
                pltpu.VMEM((n_cols, local, width), F32),
                pltpu.VMEM((n_cols, n_cols, local, piece), F32),
                pltpu.SMEM((slots,), jnp.int32),
                pltpu.SMEM((slots,), jnp.int32),
                dma((GROUPS,)),
                dma((n_cols + 2,)),
                dma((ITERS, GROUPS)),
                dma((ITERS, GROUPS)),
                dma((ITERS, GROUPS)),
                dma((ITERS, GROUPS)),
                dma((ITERS,)),
                dma((ITERS,)),
                dma((ITERS,)),
                dma((ITERS,)),
                dma((2,)),
                dma((2,)),
            ],
            compiler_params=pltpu.CompilerParams(
                collective_id=0, has_side_effects=True, vmem_limit_bytes=62 * 1024 * 1024
            ),
        )(tile_values, tile_rows, tile_cols, start_vectors)

    return jax.shard_map(
        body,
        mesh=mesh,
        in_specs=(P("rows", None, None), P("rows"), P("rows"), P("cols", "rows")),
        out_specs=(P("cols", "rows"), P("cols", "rows")),
        check_vma=False,
    )
```

```python
import functools

import jax
import jax.numpy as jnp
from jax import lax
from jax.experimental import pallas as pl
from jax.experimental.pallas import tpu as pltpu
from jax.sharding import PartitionSpec as P

REACH = 2
ITERS = 3
PARTS = 2
SUB = 8
VMEM = 62 * 1024 * 1024
GROUPS = 2 * REACH + 1
MESH = pl.DeviceIdType.MESH
F32 = jnp.float32
BF16 = jnp.bfloat16


def split(x, parts):
    out = []
    for part in range(parts):
        piece = x.astype(BF16)
        out.append(piece)
        if part < parts - 1:
            x = x - piece.astype(F32)
    return out


def dot(a, b, dims):
    return lax.dot_general(a, b, (dims, ((), ())), preferred_element_type=F32)


def dot32(a, b, dims):
    return lax.dot_general(
        a, b, (dims, ((), ())), precision=lax.Precision.HIGHEST, preferred_element_type=F32
    )


def wait_bytes(ref, sem):
    pltpu.make_async_copy(ref, ref, sem).wait()


def factor_step(bands, result, s, scale):
    count = len(bands)
    full = bands[0].shape
    lane = lax.broadcasted_iota(jnp.int32, full, 1)
    row = lax.broadcasted_iota(jnp.int32, full, 0)
    base = s * SUB
    band = bands[s]
    cols = [jnp.broadcast_to(band[:, base + k : base + k + 1], full) for k in range(SUB)]
    entry = {
        (k, l): jnp.broadcast_to(cols[l][k : k + 1], full) for k in range(SUB) for l in range(k, SUB)
    }
    follows = s + 1 < count
    if follows:
        below = bands[s + 1]
        below_cols = [jnp.broadcast_to(below[:, base + k : base + k + 1], full) for k in range(SUB)]
    inverse_rows = jnp.zeros(full, F32)
    pivots = jnp.zeros(full, F32)
    for k in range(SUB):
        inverse = pl.reciprocal(entry[k, k])
        pivots = jnp.where(row == k, entry[k, k], pivots)
        inverse_rows = jnp.where(row == k, inverse, inverse_rows)
        factors = {l: entry[k, l] * inverse for l in range(k + 1, SUB)}
        for l in range(k + 1, SUB):
            for j in range(l, SUB):
                entry[l, j] = entry[l, j] - factors[l] * entry[k, j]
        here = lane == base + k
        pivot_row = jnp.where(here, 1.0, jnp.broadcast_to(band[k : k + 1], full))
        if k < SUB - 1:
            step = jnp.where(row > k, cols[k] * inverse, 0.0)
            for l in range(k + 1, SUB):
                cols[l] = cols[l] - step * entry[k, l]
            band = jnp.where(here & (row > k), 0.0, band) - step * pivot_row
        if follows:
            step = below_cols[k] * inverse
            for l in range(k + 1, SUB):
                below_cols[l] = below_cols[l] - step * entry[k, l]
            below = jnp.where(here, 0.0, below) - step * pivot_row
    if follows:
        bands[s + 1] = below
    offset = lane - base
    if s + 2 < count:
        right = jnp.where(offset == row, 1.0, jnp.where((offset > row) & (offset < SUB), 0.0, band))
        left_parts = [part.astype(F32) for part in split(band * inverse_rows, 3)]
        right_parts = [part.astype(F32) for part in split(right, 3)]
        pairs = [(0, 0), (0, 1), (1, 0), (1, 1), (0, 2), (2, 0)]
        left_all = jnp.concatenate([left_parts[a] for a, b in pairs], axis=0).astype(BF16)
        right_all = jnp.concatenate([right_parts[b] for a, b in pairs], axis=0).astype(BF16)
        change = dot(left_all, right_all, ((0,), (0,)))
        inside = (offset >= 0) & (offset < SUB)
        for i in range(s + 2, count):
            bands[i] = jnp.where(inside, 0.0, bands[i]) - change[i * SUB : (i + 1) * SUB]
    unit = jnp.where(offset == row, 1.0, jnp.where(offset < row, band, 0.0))
    result.append(unit * (scale / jnp.sqrt(pivots)))


def kernel(
    n_rows, n_cols, scale,
    tiles_hbm, rows_hbm, cols_hbm, start,
    vectors_out, images_out,
    tiles, dense, source, window, terms, landed, gram, collected, whole_gram, all_images, all_pulled,
    tile_rows, tile_cols, tile_sem, input_sem, window_send, window_recv, terms_send, terms_recv,
    reduce_send, reduce_recv, spread_send, spread_recv, last_send, last_recv,
):
    p, c = lax.axis_index("rows"), lax.axis_index("cols")
    n_devices = n_rows * n_cols
    me = p * n_cols + c
    local, width = start.shape
    piece = width // n_cols
    size = local * n_cols
    blocks = 2
    tile = tiles.shape[1]
    in_group = tiles.shape[0] // GROUPS
    reducers = size // SUB
    stride = n_devices // reducers
    is_reducer = lax.rem(me, stride) == 0

    def at(row, col):
        return {"rows": row, "cols": col}

    def flat(index):
        return at(index // n_cols, lax.rem(index, n_cols))

    def valid(group):
        there = p + group - REACH
        return (there >= 0) & (there < n_rows)

    def copy_of_tiles(group):
        part = pl.ds(group * in_group, in_group)
        return pltpu.make_async_copy(tiles_hbm.at[part], tiles.at[part], tile_sem.at[group])

    for group in range(GROUPS):
        copy_of_tiles(group).start()

    inputs = [
        pltpu.make_async_copy(start.at[:, pl.ds(part * piece, piece)], source.at[0, part], input_sem.at[part])
        for part in range(n_cols)
    ]
    tables = [
        pltpu.make_async_copy(rows_hbm, tile_rows, input_sem.at[n_cols]),
        pltpu.make_async_copy(cols_hbm, tile_cols, input_sem.at[n_cols + 1]),
    ]
    for copy in inputs + tables:
        copy.start()

    barrier = pltpu.get_barrier_semaphore()

    def others(visit):
        def step(index, carry):
            visit(flat(lax.rem(me + index, n_devices)))
            return carry

        lax.fori_loop(1, n_devices, step, 0, unroll=n_devices <= 32)

    others(lambda device: pl.semaphore_signal(barrier, inc=1, device_id=device, device_id_type=MESH))

    for group in range(GROUPS):

        @pl.when(jnp.logical_not(valid(group)))
        def _():
            for iteration in range(ITERS):
                part = pl.ds(group * n_cols, n_cols)
                window[iteration, part] = jnp.zeros((n_cols, local, piece), F32)
                terms[iteration, part] = jnp.zeros((n_cols, local, piece), F32)

    for copy in inputs:
        copy.wait()
    pl.semaphore_wait(barrier, n_devices - 1)

    for group in range(GROUPS):
        mirror = GROUPS - 1 - group
        there = window.at[0, pl.ds(mirror * n_cols, n_cols)]
        if group == REACH:
            pltpu.make_async_copy(source.at[0], there, window_recv.at[0, mirror]).start()
        else:

            @pl.when(valid(group))
            def _():
                pltpu.make_async_remote_copy(
                    src_ref=source.at[0],
                    dst_ref=there,
                    send_sem=window_send.at[0, group],
                    recv_sem=window_recv.at[0, mirror],
                    device_id=at(p + group - REACH, c),
                    device_id_type=MESH,
                ).start()

    for copy in tables:
        copy.wait()
    chunk = 32
    chunks = tile // chunk
    for group in range(GROUPS):
        copy_of_tiles(group).wait()
        weights = []
        for r in range(blocks):
            for b in range(blocks):
                for s in range(in_group):
                    slot = group * in_group + s
                    hit = (tile_rows[slot] == r) & (lax.rem(tile_cols[slot], blocks) == b)
                    weights.append(jnp.where(hit, 1.0, 0.0).astype(F32))

        def build(index, carry):
            start_row = pl.multiple_of(index * chunk, chunk)
            values = [tiles[group * in_group + s, pl.ds(start_row, chunk), :] for s in range(in_group)]
            for r in range(blocks):
                for b in range(blocks):
                    first = (r * blocks + b) * in_group
                    total = values[0] * weights[first]
                    for s in range(1, in_group):
                        total = total + values[s] * weights[first + s]
                    for number, part in enumerate(split(total, PARTS)):
                        dense[number, group, pl.ds(r * tile + start_row, chunk), b * tile : (b + 1) * tile] = part
            return carry

        lax.fori_loop(0, chunks, build, 0)

    def product(x, group, dims):
        parts = split(x, PARTS)
        total = None
        for number in range(PARTS):
            count = PARTS
            stacked = jnp.concatenate(parts[:count], axis=0)
            result = dot(stacked, dense[number, group], dims)
            for k in range(count):
                term = result[k * local : (k + 1) * local]
                total = term if total is None else total + term
        return total

    def send_pieces(iteration, group, buffer, sources, first, send, recv):
        mirror = GROUPS - 1 - group
        slot = mirror * n_cols + c

        def remote(steps):
            for step in steps:
                col = lax.rem(c + step, n_cols)
                pltpu.make_async_remote_copy(
                    src_ref=sources.at[first + col],
                    dst_ref=buffer.at[iteration, slot],
                    send_sem=send.at[iteration, group],
                    recv_sem=recv.at[iteration, mirror],
                    device_id=at(p + group - REACH, col),
                    device_id_type=MESH,
                ).start()

        if group == REACH:
            remote(range(1, n_cols))
            pltpu.make_async_copy(
                sources.at[first + c], buffer.at[iteration, slot], recv.at[iteration, mirror]
            ).start()
        else:
            pl.when(valid(group))(functools.partial(remote, range(n_cols)))

    def spread_over_cols(src, buffer, number):
        for step in range(1, n_cols):
            pltpu.make_async_remote_copy(
                src_ref=src,
                dst_ref=buffer.at[c],
                send_sem=last_send.at[number],
                recv_sem=last_recv.at[number],
                device_id=at(p, lax.rem(c + step, n_cols)),
                device_id_type=MESH,
            ).start()
        pltpu.make_async_copy(src, buffer.at[c], last_recv.at[number]).start()

    order = [group for group in range(GROUPS) if group != REACH]
    order = sorted(order, key=lambda group: -abs(group - REACH)) + [REACH]

    def wait_group(buffer, recv, iteration, group):
        part = buffer.at[iteration, pl.ds(group * n_cols, n_cols)]
        pl.when(valid(group))(lambda: wait_bytes(part, recv.at[iteration, group]))

    def images_and_terms(iteration):
        images = jnp.zeros((local, width), F32)
        for group in reversed(order):
            wait_group(window, window_recv, iteration, group)
            near = jnp.concatenate([window[iteration, group * n_cols + k] for k in range(n_cols)], axis=1)
            images = images + product(near, group, ((1,), (1,)))
        if iteration == ITERS - 1:
            images_out[...] = images
            spread_over_cols(images_out, all_images, 0)
        def send(group):
            send_pieces(
                iteration, group, terms, landed.at[iteration], group * n_cols, terms_send, terms_recv
            )

        state = begin_factor(iteration - 1) if iteration > 0 else None
        for number, group in enumerate(order):
            pulled = product(images, group, ((1,), (0,)))
            for col in range(n_cols):
                landed[iteration, group * n_cols + col] = pulled[:, col * piece : (col + 1) * piece]
            if state is None:
                send(group)
            else:
                factor(state, 2 if number == 0 else 1)
        if state is not None:
            for group in order:
                send(group)
        return state

    def pull(iteration):
        total = None
        for group in order:
            wait_group(terms, terms_recv, iteration, group)
            part = terms[iteration, group * n_cols : (group + 1) * n_cols].reshape(size, piece)
            total = part if total is None else total + part
        return total

    def start_gram(iteration, pulled):
        gram[iteration] = dot32(pulled, pulled, ((1,), (1,)))

        def part_of(index):
            return gram.at[iteration, pl.ds(pl.multiple_of(index * SUB, SUB), SUB)]

        def send(index):
            pltpu.make_async_remote_copy(
                src_ref=part_of(index),
                dst_ref=collected.at[iteration, me],
                send_sem=reduce_send.at[iteration],
                recv_sem=reduce_recv.at[iteration],
                device_id=flat(index * stride),
                device_id_type=MESH,
            ).start()

        near = me // stride
        for step in range(1, reducers):
            send(lax.rem(near + step, reducers))
        pl.when(jnp.logical_not(is_reducer))(lambda: send(near))

        @pl.when(is_reducer)
        def _():
            pltpu.make_async_copy(part_of(near), collected.at[iteration, me], reduce_recv.at[iteration]).start()

    def spread_gram(iteration):
        @pl.when(is_reducer)
        def _():
            wait_bytes(collected.at[iteration], reduce_recv.at[iteration])
            mine = pl.ds(pl.multiple_of(me // stride * SUB, SUB), SUB)
            whole_gram[ITERS + iteration, mine] = jnp.sum(collected[iteration], axis=0)
            part = whole_gram.at[ITERS + iteration, mine]
            target = whole_gram.at[iteration, mine]

            pltpu.make_async_copy(part, target, spread_recv.at[iteration]).start()

            def send(device):
                pltpu.make_async_remote_copy(
                    src_ref=part,
                    dst_ref=target,
                    send_sem=spread_send.at[iteration],
                    recv_sem=spread_recv.at[iteration],
                    device_id=device,
                    device_id_type=MESH,
                ).start()

            others(send)

    steps = size // SUB

    def begin_factor(iteration):
        wait_bytes(whole_gram.at[iteration], spread_recv.at[iteration])
        return [whole_gram[iteration, k * SUB : (k + 1) * SUB] for k in range(steps)], []

    def factor(state, count):
        bands, result = state
        for _ in range(count):
            factor_step(bands, result, len(result), scale)

    def end_factor(state, iteration):
        factor(state, steps - len(state[1]))
        whole_gram[iteration] = jnp.concatenate(state[1], axis=0)

    for iteration in range(ITERS):
        if iteration > 0:
            spread_gram(iteration - 1)
        state = images_and_terms(iteration)
        if iteration > 0:
            end_factor(state, iteration - 1)
        pulled = pull(iteration)
        if iteration > 0:
            pulled = dot32(whole_gram[iteration - 1], pulled, ((1,), (0,)))
        source[iteration + 1] = pulled.reshape(n_cols, local, piece)
        if iteration < ITERS - 1:
            for group in order:
                send_pieces(
                    iteration + 1, group, window, source.at[iteration + 1], 0, window_send, window_recv
                )
        start_gram(iteration, pulled)
        if iteration == ITERS - 1:
            spread_over_cols(source.at[ITERS], all_pulled, 1)

    spread_gram(ITERS - 1)
    own = pl.ds(pl.multiple_of(c * local, local), local)
    wait_bytes(all_images, last_recv.at[0])
    wait_bytes(all_images.at[pl.ds(0, n_cols - 1)], last_send.at[0])
    images_out[...] = dot32(
        whole_gram[ITERS - 2, own], all_images[...].reshape(size, width), ((1,), (0,))
    )
    end_factor(begin_factor(ITERS - 1), ITERS - 1)
    wait_bytes(all_pulled, last_recv.at[1])
    mix = whole_gram[ITERS - 1, own]
    for part in range(n_cols):
        vectors_out[:, part * piece : (part + 1) * piece] = dot32(
            mix, all_pulled[part].reshape(size, piece), ((1,), (0,))
        )

    wait_bytes(all_pulled.at[pl.ds(0, n_cols - 1)], last_send.at[1])
    for iteration in range(ITERS):
        for group in range(GROUPS):
            for buffer, send in ((window, window_send), (terms, terms_send)):
                if group == REACH:
                    if buffer is window and iteration == 0:
                        continue
                    part = buffer.at[iteration, pl.ds(0, n_cols - 1)]
                    wait_bytes(part, send.at[iteration, group])
                else:
                    part = buffer.at[iteration, pl.ds(0, n_cols)]
                    pl.when(valid(group))(functools.partial(wait_bytes, part, send.at[iteration, group]))

        @pl.when(is_reducer)
        def _():
            wait_bytes(gram.at[iteration, pl.ds(0, size - SUB)], reduce_send.at[iteration])
            wait_bytes(collected.at[iteration, pl.ds(0, n_devices - 1)], spread_send.at[iteration])

        @pl.when(jnp.logical_not(is_reducer))
        def _():
            wait_bytes(gram.at[iteration], reduce_send.at[iteration])


def hand_over(vectors, images, vectors_out, images_out, sem):
    copies = [
        pltpu.make_async_copy(vectors, vectors_out, sem.at[0]),
        pltpu.make_async_copy(images, images_out, sem.at[1]),
    ]
    for copy in copies:
        copy.start()
    for copy in copies:
        copy.wait()


def solution(mesh):
    n_rows, n_cols = mesh.shape["rows"], mesh.shape["cols"]

    def body(tile_values, tile_rows, tile_cols, start_vectors):
        slots, tile = tile_values.shape[:2]
        local, width = start_vectors.shape
        size, piece = local * n_cols, width // n_cols
        scale = float((width * n_rows) ** 0.5)
        pieces = (ITERS, GROUPS * n_cols, local, piece)
        dma = pltpu.SemaphoreType.DMA
        vmem = pl.BlockSpec(memory_space=pltpu.VMEM)
        hbm = pl.BlockSpec(memory_space=pltpu.HBM)
        out = jax.ShapeDtypeStruct((local, width), F32)
        results = pl.pallas_call(
            functools.partial(kernel, n_rows, n_cols, scale),
            out_shape=(out, out),
            in_specs=[hbm, hbm, hbm, hbm],
            out_specs=(vmem, vmem),
            scratch_shapes=[
                pltpu.VMEM((slots, tile, tile), F32),
                pltpu.VMEM((PARTS, GROUPS, width, width), BF16),
                pltpu.VMEM((ITERS + 1, n_cols, local, piece), F32),
                pltpu.VMEM(pieces, F32),
                pltpu.VMEM(pieces, F32),
                pltpu.VMEM(pieces, F32),
                pltpu.VMEM((ITERS, size, size), F32),
                pltpu.VMEM((ITERS, n_rows * n_cols, SUB, size), F32),
                pltpu.VMEM((2 * ITERS, size, size), F32),
                pltpu.VMEM((n_cols, local, width), F32),
                pltpu.VMEM((n_cols, n_cols, local, piece), F32),
                pltpu.SMEM((slots,), jnp.int32),
                pltpu.SMEM((slots,), jnp.int32),
                dma((GROUPS,)),
                dma((n_cols + 2,)),
                dma((ITERS, GROUPS)),
                dma((ITERS, GROUPS)),
                dma((ITERS, GROUPS)),
                dma((ITERS, GROUPS)),
                dma((ITERS,)),
                dma((ITERS,)),
                dma((ITERS,)),
                dma((ITERS,)),
                dma((2,)),
                dma((2,)),
            ],
            compiler_params=pltpu.CompilerParams(
                collective_id=0, has_side_effects=True, vmem_limit_bytes=VMEM
            ),
        )(tile_values, tile_rows, tile_cols, start_vectors)
        anywhere = pl.BlockSpec(memory_space=pl.ANY)
        return pl.pallas_call(
            hand_over,
            out_shape=(out, out),
            in_specs=[anywhere, anywhere],
            out_specs=(anywhere, anywhere),
            scratch_shapes=[dma((2,))],
            compiler_params=pltpu.CompilerParams(vmem_limit_bytes=VMEM),
        )(*results)

    return jax.shard_map(
        body,
        mesh=mesh,
        in_specs=(P("rows", None, None), P("rows"), P("rows"), P("cols", "rows")),
        out_specs=(P("cols", "rows"), P("cols", "rows")),
        check_vma=False,
    )
```
